128 devices in a mesh: dp: 8 (over y_hi, x), ctx: 4 (over z), tensor: 4 (over y_lo, core).
Axes of the slice: x: 4, y: 4 (y_hi: 2, y_lo: 2; y = y_hi * 2 + y_lo), z: 4, core: 2. Of those that a mesh axis runs over, the one named last changes fastest.
Arguments:
- tokens: bfloat16 [8, 2048, 8192], P('dp', 'ctx'), may hold values from -16 to 16
- input_proj: bfloat16 [8192, 9216], P(('dp', 'ctx'), 'tensor'), may hold values from -0.0625 to 0.0625
- step_proj: bfloat16 [8192, 128], P(('dp', 'ctx'), 'tensor'), may hold values from -1 to 1
- conv_weight: float32 [4, 9216], P(None, 'tensor'), may hold values from -4 to 4
- conv_bias: float32 [9216], P('tensor'), may hold values from -3 to 3
- step_bias: float32 [128], P('tensor'), may hold values from -5 to -3
- head_rate: float32 [128], P('tensor'), may hold values from 0.00024414062 to 1
- state_pool: bfloat16 [16, 8192, 256], P('dp', 'tensor'), may hold values from -6 to 6
- resume_slot: int32 [8], P('dp'), may hold values from 0 to 15, as said below
- offsets: int32 [8], P('dp'), may hold values from 0 to 1535
Outputs:
- boundary_states: float32 [8, 4, 8192, 256], P('dp', 'ctx', 'tensor')
The draws below stay inside these ranges and needn't reach their ends.
Inputs may be any that keep to these rules, and one draw needn't show every extreme that they name: `resume_slot`: no two responses name the same slot.
All inputs are finite; a program needn't handle non-finite values.
Results may differ from the reference program's by a relative error of at most 0.0025.
Values may be sent and summed in bfloat16 or wider, within the bound.
No kernel may reach another device: no remote copies, remote signals or barrier semaphores. Data moves between devices by JAX's collectives and lax.ppermute only.
A program may use at most 192 MiB of HBM per device.

```python
import math
import jax
import jax.numpy as jnp
from jax import lax

D = 8192
GROUPS = 4
GROUP_HEADS = 32
P_SIZE = 64
N = 256
STRETCH_DEV = 512
HEADS = 128
FILTER_CHANNELS = 9216
STRETCH = 2048
RESPONSES = 8
PROMPTS = 16
N_CTX = 4


def span_direction(key):
    return jax.random.normal(jax.random.fold_in(key, 101), (D,), jnp.float32)


def draw_tokens(key, part):
    direction_array = span_direction(key)
    key = jax.random.fold_in(key, 1)
    base = jax.random.normal(key, (RESPONSES, STRETCH, D), jnp.float32)
    places = jax.random.randint(jax.random.fold_in(key, 2), (RESPONSES, 3), 0, STRETCH)
    hits = jnp.any(jnp.arange(STRETCH)[None, :, None] == places[:, None, :], axis=2).astype(jnp.float32)
    strength = STRETCH / 300.0 / (0.5 * math.sqrt(D))
    return jnp.clip(base + hits[:, :, None] * strength * direction_array[None, None, :], -16.0, 16.0).astype(jnp.bfloat16)


def draw_step_proj(key, part):
    direction_array = span_direction(key)
    key = jax.random.fold_in(key, 3)
    base = jax.random.normal(key, (D, HEADS), jnp.float32)
    return jnp.clip((base + 0.5 * direction_array[:, None]) / math.sqrt(D), -1.0, 1.0).astype(jnp.bfloat16)


def draw_head_rate(key, part):
    key = jax.random.fold_in(key, 4)
    unit = jax.random.uniform(key, (HEADS,), jnp.float32)
    lowest = 1.0 / STRETCH
    highest = 1.0
    return lowest * jnp.exp(unit * math.log(highest / lowest))


def draw_resume_slot(key, part):
    key = jax.random.fold_in(key, 5)
    order = jax.random.permutation(jax.random.fold_in(key, 1), RESPONSES).astype(jnp.int32)
    lower_bits = jax.random.randint(jax.random.fold_in(key, 2), (RESPONSES,), 0, 2, dtype=jnp.int32)
    lower_bits = jnp.where(order == RESPONSES - 1, 1, lower_bits).astype(jnp.int32)
    lower_bits = jnp.where(order == 0, 0, lower_bits).astype(jnp.int32)
    return (2 * order + lower_bits).astype(jnp.int32)


def place_ends(entries, key, smallest, high):
    longest = entries.shape.index(max(entries.shape))
    spots = []
    for shift in (0, 1):
        where = [jax.random.randint(jax.random.fold_in(key, axis), (), 0, length) for axis, length in enumerate(entries.shape)]
        where[longest] = (where[longest] + shift) % entries.shape[longest]
        spots.append(tuple(where))
    return entries.at[spots[0]].set(smallest).at[spots[1]].set(high)


def level_of(key, shape, pieces, smallest, largest):
    factor_of, own = 1.0, jax.random.fold_in(key, 6)
    for position, shards_of in pieces:
        steps = jnp.exp(jax.random.uniform(jax.random.fold_in(own, position), (shards_of,), jnp.float32, smallest / len(pieces), largest / len(pieces)))
        factor_of = factor_of * jnp.repeat(steps, shape[position] // shards_of).reshape([-1 if axis == position else 1 for axis in range(len(shape))])
    return factor_of


def bell_draw(rng, dims, deviation, most, pieces=(), kind=jnp.bfloat16):
    drawn = deviation * jax.random.normal(rng, dims, jnp.float32)
    if pieces:
        drawn = drawn * level_of(rng, dims, pieces, -0.22, 0.18)
    return jnp.clip(drawn, -most, most).astype(kind)


def setup_inputs(seed: int = 0) -> dict:
    key_of = jax.random.split(jax.random.key(seed), 11)
    return {
        "tokens": draw_tokens(jax.random.fold_in(key_of[10], 71), 0),
        "input_proj": bell_draw(key_of[1], (D, FILTER_CHANNELS), D ** -0.5, 0.0625, ((0, 32), (1, 4))),
        "step_proj": draw_step_proj(jax.random.fold_in(key_of[10], 71), 0),
        "conv_weight": bell_draw(key_of[3], (4, FILTER_CHANNELS), 2 ** -0.5, 4.0, ((1, 4),), jnp.float32),
        "conv_bias": bell_draw(key_of[4], (FILTER_CHANNELS,), 0.5, 3.0, ((0, 4),), jnp.float32),
        "step_bias": jnp.clip(-5.0 + 2.0 * jax.random.uniform(key_of[5], (HEADS,), jnp.float32) ** level_of(key_of[5], (HEADS,), ((0, 4),), -0.2, 0.2), -5.0, -3.0),
        "head_rate": draw_head_rate(jax.random.fold_in(key_of[10], 71), 0),
        "state_pool": bell_draw(key_of[7], (PROMPTS, HEADS * P_SIZE, N), 1.0, 6.0, ((0, 8), (1, 4))),
        "resume_slot": draw_resume_slot(jax.random.fold_in(key_of[10], 71), 0),
        "offsets": place_ends(jax.random.randint(key_of[9], (RESPONSES,), 0, 3 * STRETCH // 4), jax.random.fold_in(key_of[9], 1), 0, (3 * STRETCH // 4) - 1).astype(jnp.int32),
    }


def reference(tokens, input_proj, step_proj, conv_weight, conv_bias, step_bias, head_rate, state_pool, resume_slot, offsets):
    group_width = GROUP_HEADS * P_SIZE + N

    def one_response(inputs):
        sequence, pool_slot, start_displacement = inputs
        projected = jnp.dot(sequence, input_proj, preferred_element_type=jnp.float32).astype(jnp.bfloat16)
        step_raw = jnp.dot(sequence, step_proj, preferred_element_type=jnp.float32)
        token_places = jnp.arange(STRETCH, dtype=jnp.int32)
        is_valid = token_places >= start_displacement
        masked = jnp.where(is_valid[:, None], projected, jnp.zeros_like(projected))
        padded = jnp.concatenate([jnp.zeros((3, FILTER_CHANNELS), jnp.bfloat16), masked], axis=0).astype(jnp.float32)
        convolved = conv_bias + jnp.zeros((STRETCH, FILTER_CHANNELS), jnp.float32)
        for tap_index in range(4):
            convolved = convolved + conv_weight[tap_index] * padded[tap_index:tap_index + STRETCH]
        activated = jax.nn.silu(convolved).astype(jnp.bfloat16)
        step_size = jax.nn.softplus(step_raw + step_bias) * is_valid.astype(jnp.float32)[:, None]
        log_decay = (-head_rate * step_size).reshape(N_CTX, STRETCH_DEV, HEADS)
        running_total = jnp.cumsum(log_decay, axis=1)
        shard_total = running_total[:, -1]
        weight = jnp.exp(shard_total[:, None] - running_total) * step_size.reshape(N_CTX, STRETCH_DEV, HEADS)
        group_sorted = activated.reshape(N_CTX, STRETCH_DEV, GROUPS, group_width)
        head_inputs = group_sorted[..., :GROUP_HEADS * P_SIZE].reshape(N_CTX, STRETCH_DEV, GROUPS, GROUP_HEADS, P_SIZE)
        state_inputs = group_sorted[..., GROUP_HEADS * P_SIZE:]
        scaled = (head_inputs.astype(jnp.float32) * weight.reshape(N_CTX, STRETCH_DEV, GROUPS, GROUP_HEADS, 1)).astype(jnp.bfloat16)
        within_segment_addend = jnp.einsum('clghp,clgn->cghpn', scaled.astype(jnp.float32), state_inputs.astype(jnp.float32))
        within_segment_addend = within_segment_addend.reshape(N_CTX, HEADS * P_SIZE, N)
        shard_decay = jnp.repeat(jnp.exp(shard_total), P_SIZE, axis=1)
        initial = lax.dynamic_index_in_dim(state_pool, pool_slot, 0, keepdims=False).astype(jnp.float32)

        def advance(inherited_memory, element):
            factor, addend = element
            inherited_memory = factor[:, None] * inherited_memory + addend
            return inherited_memory, inherited_memory

        unused, bounds = lax.scan(advance, initial, (shard_decay, within_segment_addend))
        return bounds

    return lax.map(one_response, (tokens, resume_slot, offsets))
```

```python
import jax
import jax.numpy as jnp
from jax import lax
from jax.experimental import pallas as pl
from jax.experimental.pallas import tpu as pltpu
from jax.sharding import Mesh
from jax.sharding import PartitionSpec as P

GROUP_HEADS = 32
P_SIZE = 64
N = 256
HALO = 16
ROWS = 512
LONG = ROWS + HALO
PIECE = 256
HEAD_COLUMNS = GROUP_HEADS * P_SIZE
F32 = jnp.float32
BF16 = jnp.bfloat16
VMEM_LIMIT = 56 * 1024 * 1024

CHUNKS = (
    ("x", HEAD_COLUMNS, 256),
    ("z", 0, 512),
    ("x", 512, 384),
    ("z", 896, 512),
    ("x", 1408, 256),
    ("z", 1664, 384),
)


def opposed(axis, size=4):
    pairs = []
    for i in range(size):
        pairs.append((2 * i, 2 * ((i + 1) % size)))
        pairs.append((2 * i + 1, 2 * ((i - 1) % size) + 1))
    return (axis, "core"), pairs


def ring(part, axis):
    axes, pairs = opposed(axis)
    parts = [part]
    for _ in range(3):
        parts.append(lax.ppermute(parts[-1], axes, pairs))
    return parts


def ring_places(axis):
    me = lax.axis_index(axis)
    way = 1 - 2 * lax.axis_index("core")
    return [(me - way * i) % 4 for i in range(4)]


def in_order(parts, places):
    rows = parts[0].shape[0]
    whole = jnp.zeros((4 * rows,) + parts[0].shape[1:], parts[0].dtype)
    for part, place in zip(parts, places):
        whole = lax.dynamic_update_slice_in_dim(whole, part, place * rows, 0)
    return whole


def gather_weights(part, order):
    other = {"x": "z", "z": "x"}[order]
    block = in_order(ring(part, order), ring_places(order))
    return ring(block, other), jnp.stack(ring_places(other)).astype(jnp.int32)


def project_kernel(order, places_ref, own_ref, theirs_ref, w0, w1, w2, w3, own_out, theirs_out, own_acc, theirs_acc):
    for j, w_ref in enumerate((w0, w1, w2, w3)):
        place = places_ref[j]
        w = w_ref[...]
        for tokens_ref, acc in ((own_ref, own_acc), (theirs_ref, theirs_acc)):
            if order == "z":
                lhs = tokens_ref[place]
            else:
                columns = pl.ds(pl.multiple_of(place * PIECE, PIECE), PIECE)
                lhs = jnp.concatenate([tokens_ref[x, :, columns] for x in range(4)], axis=1)
            product = jnp.dot(lhs, w, preferred_element_type=F32)
            if j == 0:
                acc[...] = product
            else:
                acc[...] += product
    own_out[...] = own_acc[...]
    theirs_out[...] = theirs_acc[...].astype(theirs_out.dtype)


def project(order, own, theirs, blocks, places):
    width = blocks[0].shape[1]
    full = lambda shape: pl.BlockSpec(shape, lambda: (0,) * len(shape))
    return pl.pallas_call(
        lambda *refs: project_kernel(order, *refs),
        out_shape=(jax.ShapeDtypeStruct((LONG, width), F32), jax.ShapeDtypeStruct((LONG, width), BF16 if width % 128 == 0 else F32)),
        in_specs=[pl.BlockSpec(memory_space=pltpu.SMEM), full(own.shape), full(theirs.shape)] + [full(blocks[0].shape)] * 4,
        out_specs=(full((LONG, width)), full((LONG, width))),
        scratch_shapes=[pltpu.VMEM((LONG, width), F32), pltpu.VMEM((LONG, width), F32)],
        compiler_params=pltpu.CompilerParams(vmem_limit_bytes=VMEM_LIMIT),
        cost_estimate=pl.CostEstimate(flops=2 * 2 * LONG * 4096 * width, bytes_accessed=8_700_000 + 8192 * width, transcendentals=0),
        name="project",
    )(places, own, theirs, *blocks)


def activate(info_ref, own_ref, other_ref, taps_ref, bias_ref, masked):
    projected = (own_ref[...] + other_ref[...].astype(F32)).astype(BF16).astype(F32)
    place = info_ref[0] + lax.broadcasted_iota(jnp.int32, projected.shape, 0)
    masked[...] = jnp.where(place >= info_ref[1], projected, 0.0)
    total = bias_ref[...]
    for k in range(4):
        total = total + taps_ref[k : k + 1, :] * masked[pl.ds(HALO - 3 + k, ROWS), :]
    return (total * jax.nn.sigmoid(total)).astype(BF16)


def state_kernel(info_ref, own_ref, other_ref, taps_ref, bias_ref, out_ref, masked):
    out_ref[...] = activate(info_ref, own_ref, other_ref, taps_ref, bias_ref, masked)


def head_kernel(first_head, info_ref, own_ref, other_ref, taps_ref, bias_ref, weight_ref, states_ref, out_ref, masked):
    activated = activate(info_ref, own_ref, other_ref, taps_ref, bias_ref, masked).astype(F32)
    width = activated.shape[1]
    lane = lax.broadcasted_iota(jnp.int32, (ROWS, 128), 1)
    scaled = []
    for i in range(width // 128):
        head = first_head + 2 * i
        factor = jnp.where(lane < P_SIZE, weight_ref[:, head : head + 1], weight_ref[:, head + 1 : head + 2])
        scaled.append((activated[:, i * 128 : (i + 1) * 128] * factor).astype(BF16))
    scaled = jnp.concatenate(scaled, axis=1)
    out_ref[...] = lax.dot_general(scaled, states_ref[...], (((0,), (0,)), ((), ())), preferred_element_type=F32)


def call(kernel, out, width, *args):
    full = lambda a: pl.BlockSpec(a.shape, lambda: (0,) * len(a.shape))
    return pl.pallas_call(
        kernel,
        out_shape=out,
        in_specs=[pl.BlockSpec(memory_space=pltpu.SMEM)] + [full(a) for a in args[1:]],
        out_specs=full(out),
        scratch_shapes=[pltpu.VMEM((LONG, width), F32)],
        compiler_params=pltpu.CompilerParams(vmem_limit_bytes=VMEM_LIMIT),
        cost_estimate=pl.CostEstimate(flops=2 * ROWS * N * width, bytes_accessed=8 * LONG * width, transcendentals=ROWS * width),
        name="activate",
    )(*args)


def swap(value, axis):
    return lax.ppermute(value, axis, [(0, 1), (1, 0)])


def partner_tokens(extended):
    yh, yl, core = (lax.axis_index(a) for a in ("yh", "yl", "core"))
    quarter = 2 * (1 - yl) + core
    sent = lax.dynamic_slice(extended, (0, (1 - yh) * 4096 + quarter * 1024), (LONG, 1024))
    across = [(0, 3), (1, 2), (2, 1), (3, 0)]
    whole = jnp.zeros((4, LONG, 1024), extended.dtype)
    for first in (0, 512):
        near = lax.ppermute(sent[:, first : first + 512], ("yh", "yl"), across)
        far = swap(near, "yl")
        both = jnp.stack([near, far])
        others = swap(both, "core")
        for value, q in (
            (both[0], 2 * yl + core),
            (both[1], 2 * (1 - yl) + core),
            (others[0], 2 * yl + 1 - core),
            (others[1], 2 * (1 - yl) + 1 - core),
        ):
            whole = lax.dynamic_update_slice(whole, value[None], (q, 0, first))
    return whole


def starting_state(state_pool, resume_slot):
    yh, x, z = (lax.axis_index(a) for a in ("yh", "x", "z"))
    quarter = lax.dynamic_slice_in_dim(state_pool, z * 512, 512, 1)
    other = swap(quarter, "yh")
    slots = []
    for side, value in ((yh, quarter), (1 - yh, other)):
        for b in range(2):
            slots.append((2 * (side * 4 + x) + b, value[b]))
    found = jnp.zeros((512, N), BF16)
    for s in range(4):
        wanted = resume_slot[0]
        if s:
            wanted = lax.ppermute(resume_slot, "x", [(i, (i - s) % 4) for i in range(4)])[0]
        sent = jnp.zeros((512, N), BF16)
        for slot, value in slots:
            sent = jnp.where(wanted == slot, value, sent)
        if s:
            sent = lax.ppermute(sent, "x", [(i, (i + s) % 4) for i in range(4)])
        found = found + sent
    parts = [found] + [lax.ppermute(found, "z", [(k, 0)]) for k in (1, 2, 3)]
    return jnp.concatenate(parts, axis=0)


def per_device(tokens, input_proj, step_proj, conv_weight, conv_bias, step_bias, head_rate, state_pool, resume_slot, offsets):
    yh, z = lax.axis_index("yh"), lax.axis_index("z")
    rows = tokens[0]
    halo = lax.ppermute(rows[ROWS - HALO :], "z", [(0, 1), (1, 2), (2, 3)])
    extended = jnp.concatenate([halo, rows], axis=0)
    mine = lax.dynamic_slice_in_dim(extended, yh * 4096, 4096, 1)
    mine = jnp.stack([mine[:, x * 1024 : (x + 1) * 1024] for x in range(4)])
    theirs = partner_tokens(extended)
    info = jnp.stack([z * ROWS - HALO, offsets[0]]).astype(jnp.int32)
    initial = starting_state(state_pool, resume_slot)

    states = weight = decay = None
    pieces = {}
    for order, first, width in CHUNKS:
        part = input_proj[:, first : first + width]
        taps, bias = conv_weight[:, first : first + width], conv_bias[None, first : first + width]
        if first == HEAD_COLUMNS:
            part = jnp.concatenate([part, step_proj, jnp.zeros((PIECE, 96), BF16)], axis=1)
        blocks, places = gather_weights(part, order)
        own, theirs_part = project(order, mine, theirs, blocks, places) if first != HEAD_COLUMNS else project_with_steps(order, mine, theirs, blocks, places)
        if first == HEAD_COLUMNS:
            sent, sent_steps = theirs_part
            other = swap(sent, "yh")
            step_raw = (own[:, N : N + GROUP_HEADS] + swap(sent_steps, "yh"))[HALO:]
            states = call(state_kernel, jax.ShapeDtypeStruct((ROWS, N), BF16), N, info, own[:, :N], other, taps, bias)
            valid = (z * ROWS + jnp.arange(ROWS, dtype=jnp.int32) >= offsets[0]).astype(F32)
            step_size = jax.nn.softplus(step_raw + step_bias) * valid[:, None]
            log_decay = -head_rate * step_size
            running = jnp.cumsum(log_decay, axis=0)
            weight = jnp.exp(running[-1:] - running) * step_size
            decay = jnp.exp(running[-1])
            continue
        other = swap(theirs_part, "yh")
        head = first // P_SIZE
        heads = width // P_SIZE
        local = call(
            lambda *refs, head=head: head_kernel(head, *refs),
            jax.ShapeDtypeStruct((width, N), F32), width, info, own, other, taps, bias, weight, states,
        )
        factor = jnp.repeat(decay[head : head + heads], P_SIZE)[:, None]
        carry = initial[first : first + width]
        for k in range(3):
            state = (factor * carry.astype(F32) + local).astype(BF16)
            came = lax.ppermute(state, "z", [(k, k + 1)])
            carry = jnp.where(z == k + 1, came, carry)
        pieces[first] = factor * carry.astype(F32) + local
    return jnp.concatenate([pieces[f] for f in sorted(pieces)], axis=0)[None, None]


def project_with_steps(order, own, theirs, blocks, places):
    width = blocks[0].shape[1]
    full = lambda shape: pl.BlockSpec(shape, lambda: (0,) * len(shape))

    def kernel(places_ref, own_ref, theirs_ref, w0, w1, w2, w3, own_out, states_out, steps_out, own_acc, theirs_acc, all_out):
        project_kernel(order, places_ref, own_ref, theirs_ref, w0, w1, w2, w3, own_out, all_out, own_acc, theirs_acc)
        states_out[...] = all_out[:, :N].astype(BF16)
        steps_out[...] = all_out[:, N : N + GROUP_HEADS]

    own_out, states_out, steps_out = pl.pallas_call(
        kernel,
        out_shape=(
            jax.ShapeDtypeStruct((LONG, width), F32),
            jax.ShapeDtypeStruct((LONG, N), BF16),
            jax.ShapeDtypeStruct((LONG, GROUP_HEADS), F32),
        ),
        in_specs=[pl.BlockSpec(memory_space=pltpu.SMEM), full(own.shape), full(theirs.shape)] + [full(blocks[0].shape)] * 4,
        out_specs=(full((LONG, width)), full((LONG, N)), full((LONG, GROUP_HEADS))),
        scratch_shapes=[pltpu.VMEM((LONG, width), F32)] * 3,
        compiler_params=pltpu.CompilerParams(vmem_limit_bytes=VMEM_LIMIT),
        cost_estimate=pl.CostEstimate(flops=2 * 2 * LONG * 4096 * width, bytes_accessed=8_700_000 + 8192 * width, transcendentals=0),
        name="project_steps",
    )(places, own, theirs, *blocks)
    return own_out, (states_out, steps_out)


def solution(mesh):
    fine = Mesh(mesh.devices.reshape(2, 4, 4, 2, 2), ("yh", "x", "z", "yl", "core"))
    dp, tensor = ("yh", "x"), ("yl", "core")
    return jax.shard_map(
        per_device,
        mesh=fine,
        in_specs=(
            P(dp, "z", None),
            P(dp + ("z",), tensor),
            P(dp + ("z",), tensor),
            P(None, tensor),
            P(tensor),
            P(tensor),
            P(tensor),
            P(dp, tensor, None),
            P(dp),
            P(dp),
        ),
        out_specs=P(dp, "z", tensor, None),
        check_vma=False,
    )
```

```python
import jax
import jax.numpy as jnp
from jax import lax
from jax.experimental import pallas as pl
from jax.experimental.pallas import tpu as pltpu
from jax.sharding import Mesh
from jax.sharding import PartitionSpec as P

GROUP_HEADS = 32
P_SIZE = 64
N = 256
HALO = 16
ROWS = 512
LONG = ROWS + HALO
PIECE = 256
HALF = 4096
HEAD_COLUMNS = GROUP_HEADS * P_SIZE
F32 = jnp.float32
BF16 = jnp.bfloat16
VMEM_LIMIT = 48 * 1024 * 1024
VMEM = pl.BlockSpec(memory_space=pltpu.VMEM)
SMEM = pl.BlockSpec(memory_space=pltpu.SMEM)
ANY = pl.BlockSpec(memory_space=pltpu.HBM)

CHUNKS = {
    "states": (HEAD_COLUMNS, 256),
    "a": (0, 512),
    "b": (512, 512),
    "c": (1024, 512),
    "d": (1536, 512),
}


def together(*values):
    return lax.optimization_barrier(values)


def shifted(part, axis, by):
    return lax.ppermute(part, axis, [(i, (i + by) % 4) for i in range(4)])


def ring_places():
    x, z = lax.axis_index("x"), lax.axis_index("z")
    index = jnp.arange(16, dtype=jnp.int32)
    step = lambda i: jnp.where(i == 1, 3, jnp.where(i == 2, 1, jnp.where(i == 3, 2, 0)))
    outer, inner = step(index // 4), step(index % 4)
    return (x + inner) % 4 * 4 + (z + outer) % 4, index


def params():
    return pltpu.CompilerParams(vmem_limit_bytes=VMEM_LIMIT)


def pile(parts):
    width = parts[0].shape[1]
    heights = [part.shape[0] for part in parts]

    def kernel(*refs):
        copies = [
            pltpu.make_async_copy(ref, refs[len(parts)].at[pl.ds(sum(heights[:i]), heights[i])], refs[-1].at[i])
            for i, ref in enumerate(refs[: len(parts)])
        ]
        for copy in copies:
            copy.start()
        for copy in copies:
            copy.wait()

    whole = (sum(heights), width)
    return pl.pallas_call(
        kernel,
        out_shape=jax.ShapeDtypeStruct(whole, parts[0].dtype),
        in_specs=[ANY] * len(parts),
        out_specs=VMEM,
        scratch_shapes=[pltpu.SemaphoreType.DMA((len(parts),))],
        compiler_params=params(),
        cost_estimate=pl.CostEstimate(flops=0, bytes_accessed=4 * whole[0] * width, transcendentals=0),
        name="pile",
    )(*parts)


def cut(rows, first, width, pool=None, row=None):
    def kernel(at_ref, rows_ref, *refs):
        out, sems = refs[-2:]
        parts = [(rows_ref.at[:, pl.ds(pl.multiple_of(at_ref[0], PIECE), width)], out.at[:, pl.ds(0, width)])]
        if pool is not None:
            for slot in range(2):
                source = refs[0].at[slot, pl.ds(pl.multiple_of(at_ref[1], 512), 512)]
                parts.append((source, out.at[:, pl.ds(width + slot * N, N)]))
        copies = [pltpu.make_async_copy(source, target, sems.at[i]) for i, (source, target) in enumerate(parts)]
        for copy in copies:
            copy.start()
        for copy in copies:
            copy.wait()

    with_pool = pool is not None
    whole = width + 2 * N if with_pool else width
    return pl.pallas_call(
        kernel,
        out_shape=jax.ShapeDtypeStruct((rows.shape[0], whole), rows.dtype),
        in_specs=[SMEM, ANY] + [ANY] * with_pool,
        out_specs=VMEM,
        scratch_shapes=[pltpu.SemaphoreType.DMA((3,))],
        compiler_params=params(),
        cost_estimate=pl.CostEstimate(flops=0, bytes_accessed=4 * rows.shape[0] * whole, transcendentals=0),
        name="cut",
    )(jnp.stack([first, row if with_pool else first]).astype(jnp.int32), rows, *([pool] if with_pool else []))


NEAR = (768, 1280)


def in_blocks(name, pick, halo, at, *sources):
    def kernel(at_ref, halo_ref, *refs):
        out_ref, sems = refs[len(sources) :]
        parts = [(halo_ref, out_ref.at[:, pl.ds(0, HALO)])]
        for i in range(16):
            source, place = pick(at_ref, refs, i)
            parts.append((source, out_ref.at[place, pl.ds(HALO, ROWS)]))
        copies = [pltpu.make_async_copy(source, target, sems.at[i]) for i, (source, target) in enumerate(parts)]
        for copy in copies:
            copy.start()
        for copy in copies:
            copy.wait()

    return pl.pallas_call(
        kernel,
        out_shape=jax.ShapeDtypeStruct((16, LONG, PIECE), halo.dtype),
        in_specs=[SMEM] + [ANY] * (1 + len(sources)),
        out_specs=VMEM,
        scratch_shapes=[pltpu.SemaphoreType.DMA((17,))],
        compiler_params=params(),
        cost_estimate=pl.CostEstimate(flops=0, bytes_accessed=4 * LONG * HALF, transcendentals=0),
        name=name,
    )(at[None].astype(jnp.int32), halo, *sources)


def own_tokens(rows, halo):
    def pick(at_ref, refs, i):
        return refs[0].at[:, pl.ds(pl.multiple_of(at_ref[0] * HALF + i * PIECE, PIECE), PIECE)], i

    return in_blocks("own_tokens", pick, halo, lax.axis_index("yh"), rows)


def partner_tokens(nears, fars, halo):
    def pick(at_ref, refs, i):
        place = at_ref[0] * 8 + i if i < 8 else (1 - at_ref[0]) * 8 + i - 8
        begin, piece = i % 8 * PIECE, 0
        if begin >= NEAR[0]:
            begin, piece = begin - NEAR[0], 1
        return refs[i // 8 * 2 + piece].at[:, pl.ds(begin, PIECE)], place

    return in_blocks("partner_tokens", pick, halo, lax.axis_index("core"), *nears, *fars)


def project(own, theirs, blocks, places, first, width, steps):
    n_blocks = len(blocks)

    def kernel(places_ref, *refs):
        sides, w_refs, outs, refs = refs[:2], refs[2 : 2 + n_blocks], refs[2 + n_blocks : 4 + n_blocks], refs[4 + n_blocks :]
        accs, held, sems = refs[:2], refs[2], refs[3]
        copies = []
        for j in range(4):
            row = pl.ds(j * 1024, 1024)
            source = w_refs[0].at[row, pl.ds(first, width)] if n_blocks == 1 else w_refs[j]
            copies.append(pltpu.make_async_copy(source, held.at[row], sems.at[j]))
            copies[j].start()
        for j in range(4):
            copies[j].wait()
            w = held[j * 1024 : (j + 1) * 1024]
            for side in range(2):
                lhs = jnp.concatenate([sides[side][places_ref[4 * j + i]] for i in range(4)], axis=1)
                product = jnp.dot(lhs, w, preferred_element_type=F32)
                if j == 0:
                    accs[side][...] = product
                elif j < 3:
                    accs[side][...] += product
                elif side == 0:
                    outs[0][...] = accs[0][...] + product
                else:
                    total = accs[1][...] + product
                    if steps:
                        outs[1][:, :N] = total[:, :N].astype(BF16)
                        exact = total[:, N:]
                        high = exact.astype(BF16)
                        outs[1][:, N : N + 128] = high
                        outs[1][:, N + 128 :] = (exact - high.astype(F32)).astype(BF16)
                    else:
                        outs[1][...] = total.astype(BF16)

    their_width = width + 128 if steps else width
    return pl.pallas_call(
        kernel,
        out_shape=(jax.ShapeDtypeStruct((LONG, width), F32), jax.ShapeDtypeStruct((LONG, their_width), BF16)),
        in_specs=[SMEM, VMEM, VMEM] + [ANY] * n_blocks,
        out_specs=(VMEM, VMEM),
        scratch_shapes=[pltpu.VMEM((LONG, width), F32)] * 2 + [pltpu.VMEM((HALF, width), BF16), pltpu.SemaphoreType.DMA((4,))],
        compiler_params=params(),
        cost_estimate=pl.CostEstimate(flops=4 * LONG * HALF * width, bytes_accessed=8192 * width, transcendentals=0),
        name="project",
    )(places, own, theirs, *blocks)


def activate(info_ref, projected, taps_ref, bias_ref, first, masked):
    projected = projected.astype(BF16).astype(F32)
    place = info_ref[0] + lax.broadcasted_iota(jnp.int32, projected.shape, 0)
    masked[...] = jnp.where(place >= info_ref[1], projected, 0.0)
    columns = slice(first, first + projected.shape[1])
    total = bias_ref[:, columns]
    for k in range(4):
        total = total + taps_ref[k : k + 1, columns] * masked[pl.ds(HALO - 3 + k, ROWS), :]
    return (total * jax.nn.sigmoid(total)).astype(BF16)


def state_kernel(info_ref, own_ref, other_ref, taps_ref, bias_ref, states_out, steps_out, masked):
    projected = own_ref[:, :N] + other_ref[:, :N].astype(F32)
    states_out[...] = activate(info_ref, projected, taps_ref, bias_ref, HEAD_COLUMNS, masked)
    steps = own_ref[HALO:, N : N + 128] + other_ref[HALO:, N : N + 128].astype(F32) + other_ref[HALO:, N + 128 :].astype(F32)
    steps_out[...] = steps[:, :GROUP_HEADS]


def head_kernel(first_head, info_ref, own_ref, other_ref, taps_ref, bias_ref, weight_ref, states_ref, out_ref, masked):
    projected = own_ref[...] + other_ref[...].astype(F32)
    activated = activate(info_ref, projected, taps_ref, bias_ref, first_head * P_SIZE, masked).astype(F32)
    lane = lax.broadcasted_iota(jnp.int32, (ROWS, 128), 1)
    scaled = []
    for i in range(activated.shape[1] // 128):
        head = first_head + 2 * i
        factor = jnp.where(lane < P_SIZE, weight_ref[:, head : head + 1], weight_ref[:, head + 1 : head + 2])
        scaled.append((activated[:, i * 128 : (i + 1) * 128] * factor).astype(BF16))
    scaled = jnp.concatenate(scaled, axis=1)
    out_ref[...] = lax.dot_general(scaled, states_ref[...], (((0,), (0,)), ((), ())), preferred_element_type=F32)


def call(kernel, out, width, *args):
    return pl.pallas_call(
        kernel,
        out_shape=out,
        in_specs=[SMEM] + [VMEM] * (len(args) - 1),
        out_specs=jax.tree.map(lambda _: VMEM, out),
        scratch_shapes=[pltpu.VMEM((LONG, width), F32)],
        compiler_params=params(),
        cost_estimate=pl.CostEstimate(flops=2 * ROWS * N * width, bytes_accessed=8 * LONG * width, transcendentals=ROWS * width),
        name="activate",
    )(*args)


def swap(value, axis):
    return lax.ppermute(value, axis, [(0, 1), (1, 0)])


def halos(rows):
    yh = lax.axis_index("yh")
    last = rows[ROWS - HALO :].reshape(HALO, 2, 16, PIECE).transpose(1, 2, 0, 3)
    mine = lax.ppermute(lax.dynamic_index_in_dim(last, yh, 0, False), "z", [(0, 1), (1, 2), (2, 3)])
    pairs = [(y * 4 + z, (1 - y) * 4 + z + 1) for y in range(2) for z in range(3)]
    return mine, lax.ppermute(lax.dynamic_index_in_dim(last, 1 - yh, 0, False), ("yh", "z"), pairs)


def behind(value, by):
    return lax.ppermute(value, "z", [(i, i + by) for i in range(4 - by)])


def saved_state(near, far, wanted):
    yh, x = lax.axis_index("yh"), lax.axis_index("x")
    slots = []
    for side, value in ((yh, near), (1 - yh, far)):
        for b in range(2):
            slots.append((2 * (side * 4 + x) + b, value[:, NEAR[1] + b * N : NEAR[1] + (b + 1) * N]))
    sent = []
    for i in range(4):
        picked = jnp.zeros((512, N), BF16)
        for slot, value in slots:
            picked = jnp.where(wanted[i] == slot, value, picked)
        sent.append(picked)
    return sent


def per_device(tokens, input_proj, step_proj, conv_weight, conv_bias, step_bias, head_rate, state_pool, resume_slot, offsets):
    yh, x, z, core = (lax.axis_index(a) for a in ("yh", "x", "z", "core"))
    rows = tokens[0]
    info = jnp.stack([z * ROWS - HALO, offsets[0]]).astype(jnp.int32)

    x_first, in_order = together(*ring_places())
    slot = jnp.broadcast_to(resume_slot[0].astype(BF16), (PIECE, 1))
    s = jnp.concatenate([input_proj[:, HEAD_COLUMNS:], step_proj, slot, jnp.zeros((PIECE, 95), BF16)], axis=1)
    half = (1 - yh) * HALF + core * 2048
    gathered = lax.all_gather(input_proj[:, :HEAD_COLUMNS], ("x", "z"), axis=0, tiled=True)

    first_piece = cut(rows, half, NEAR[0])
    s, first_piece = together(s, first_piece)
    first_near = swap(first_piece, "yh")
    second_piece = cut(rows, half + NEAR[0], NEAR[1], state_pool, z * 512)
    around = [shifted(s, "x", by) for by in (1, -1, 2)]
    my_halo, their_halo = halos(rows)
    *around, first_near, second_piece, my_halo, their_halo = together(*around, first_near, second_piece, my_halo, their_halo)
    second_near = swap(second_piece, "yh")
    s = pile([s, *around])
    around = [shifted(s, "z", by) for by in (1, -1, 2)]
    first_far = swap(first_near, "core")
    own_side = own_tokens(rows, my_halo)
    s, *around, second_near, first_far, own_side = together(s, *around, second_near, first_far, own_side)
    s = [s, *around]
    second_far = swap(second_near[:, : NEAR[1]], "core")
    partner_side = partner_tokens((first_near, second_near), (first_far, second_far), their_halo)
    projected = {}

    def run(name, blocks, places):
        first, width = CHUNKS[name]
        steps = name == "states"
        own, sent = project(own_side, partner_side, blocks, places, first, width + 128 if steps else width, steps)
        projected[name] = [own, swap(sent, "yh")]

    run("states", s, x_first)
    wanted = [s[0][PIECE * i, N + GROUP_HEADS].astype(jnp.int32) for i in (0, 2, 3, 1)]
    picked = saved_state(second_piece, second_near, wanted)
    found = [picked[0]] + [shifted(picked[i], "x", i) for i in (1, 2, 3)]
    out = (jax.ShapeDtypeStruct((ROWS, N), BF16), jax.ShapeDtypeStruct((ROWS, GROUP_HEADS), F32))
    states, step_raw = call(state_kernel, out, N, info, *projected["states"], conv_weight, conv_bias[None])

    valid = (z * ROWS + jnp.arange(ROWS, dtype=jnp.int32) >= offsets[0]).astype(F32)
    step_size = jax.nn.softplus(step_raw + step_bias) * valid[:, None]
    log_decay = -head_rate * step_size
    running = jnp.cumsum(log_decay, axis=0)
    weight = jnp.exp(running[-1:] - running) * step_size
    decay = jnp.exp(running[-1])
    before = behind(decay, 1)
    factors = [jnp.repeat(f, P_SIZE)[:, None] for f in (decay, decay * before)]

    found = found[0] + found[1] + found[2] + found[3]
    initial = jnp.concatenate([found] + [lax.ppermute(found, "z", [(k, 0)]) for k in (1, 2, 3)], axis=0)
    start = jnp.where(z == 0, factors[0] * initial.astype(F32), 0.0)
    gathered, weight, states, start, *factors = together(gathered, weight, states, start, *factors)

    def head(name):
        first, width = CHUNKS[name]
        kernel = lambda *refs: head_kernel(first // P_SIZE, *refs)
        out = jax.ShapeDtypeStruct((width, N), F32)
        return call(kernel, out, width, info, *projected[name], conv_weight, conv_bias[None], weight, states)

    local = {}
    run("a", [gathered], in_order)
    run("b", [gathered], in_order)
    gathered, projected["a"][1] = together(gathered, projected["a"][1])
    run("c", [gathered], in_order)
    projected["a"][0], projected["c"][0] = together(projected["a"][0], projected["c"][0])
    local["a"] = head("a")
    gathered, projected["b"][1], local["a"] = together(gathered, projected["b"][1], local["a"])
    run("d", [gathered], in_order)
    projected["b"][0], projected["d"][0], local["a"] = together(projected["b"][0], projected["d"][0], local["a"])
    local["b"] = head("b")
    result = []
    for names in (("a", "b"), ("c",), ("d",)):
        first = CHUNKS[names[0]][0]
        last = first + sum(CHUNKS[name][1] for name in names)
        own = jnp.concatenate([local[name] if name in local else head(name) for name in names], axis=0) + start[first:last]
        for factor, by in zip(factors, (1, 2)):
            own = own + factor[first:last] * behind(own.astype(BF16), by).astype(F32)
        result.append(own)
    return jnp.concatenate(result, axis=0)[None, None]


def solution(mesh):
    fine = Mesh(mesh.devices.reshape(2, 4, 4, 2, 2), ("yh", "x", "z", "yl", "core"))
    dp, tensor = ("yh", "x"), ("yl", "core")
    return jax.shard_map(
        per_device,
        mesh=fine,
        in_specs=(
            P(dp, "z", None),
            P(dp + ("z",), tensor),
            P(dp + ("z",), tensor),
            P(None, tensor),
            P(tensor),
            P(tensor),
            P(tensor),
            P(dp, tensor, None),
            P(dp),
            P(dp),
        ),
        out_specs=P(dp, "z", tensor, None),
        check_vma=False,
    )
```

```python
import jax
import jax.numpy as jnp
from jax import lax
from jax.experimental import pallas as pl
from jax.experimental.pallas import tpu as pltpu
from jax.sharding import Mesh
from jax.sharding import PartitionSpec as P

GROUP_HEADS = 32
P_SIZE = 64
N = 256
HALO = 16
ROWS = 512
LONG = ROWS + HALO
PIECE = 256
HALF = 4096
HEAD_COLUMNS = GROUP_HEADS * P_SIZE
F32 = jnp.float32
BF16 = jnp.bfloat16
VMEM_LIMIT = 60 * 1024 * 1024
VMEM = pl.BlockSpec(memory_space=pltpu.VMEM)
SMEM = pl.BlockSpec(memory_space=pltpu.SMEM)
ANY = pl.BlockSpec(memory_space=pltpu.HBM)

CHUNKS = {
    "states": (HEAD_COLUMNS, 256),
    "a": (0, 768),
    "b": (768, 768),
    "c": (1536, 512),
}
SPLIT = 1536
STATE_WIDTH = 384


def together(*values):
    return lax.optimization_barrier(values)


def shifted(part, axis, by):
    return lax.ppermute(part, axis, [(i, (i + by) % 4) for i in range(4)])


def params():
    return pltpu.CompilerParams(vmem_limit_bytes=VMEM_LIMIT)


def pile(parts):
    width = parts[0].shape[1]
    heights = [part.shape[0] for part in parts]

    def kernel(*refs):
        copies = [
            pltpu.make_async_copy(ref, refs[len(parts)].at[pl.ds(sum(heights[:i]), heights[i])], refs[-1].at[i])
            for i, ref in enumerate(refs[: len(parts)])
        ]
        for copy in copies:
            copy.start()
        for copy in copies:
            copy.wait()

    whole = (sum(heights), width)
    return pl.pallas_call(
        kernel,
        out_shape=jax.ShapeDtypeStruct(whole, parts[0].dtype),
        in_specs=[ANY] * len(parts),
        out_specs=VMEM,
        scratch_shapes=[pltpu.SemaphoreType.DMA((len(parts),))],
        compiler_params=params(),
        cost_estimate=pl.CostEstimate(flops=0, bytes_accessed=4 * whole[0] * width, transcendentals=0),
        name="pile",
    )(*parts)


def cut(rows, first, width):
    def kernel(first_ref, rows_ref, out_ref, sem):
        copy = pltpu.make_async_copy(rows_ref.at[:, pl.ds(pl.multiple_of(first_ref[0], PIECE), width)], out_ref, sem)
        copy.start()
        copy.wait()

    return pl.pallas_call(
        kernel,
        out_shape=jax.ShapeDtypeStruct((rows.shape[0], width), rows.dtype),
        in_specs=[SMEM, ANY],
        out_specs=VMEM,
        scratch_shapes=[pltpu.SemaphoreType.DMA],
        compiler_params=params(),
        cost_estimate=pl.CostEstimate(flops=0, bytes_accessed=4 * rows.shape[0] * width, transcendentals=0),
        name="cut",
    )(first[None].astype(jnp.int32), rows)


NEAR = (768, 1280)


def in_blocks(name, pick, halo, at, *sources):
    def kernel(at_ref, halo_ref, *refs):
        out_ref, sems = refs[len(sources) :]
        parts = [(halo_ref, out_ref.at[:, pl.ds(0, HALO)])]
        for i in range(16):
            source, place = pick(at_ref, refs, i)
            parts.append((source, out_ref.at[place, pl.ds(HALO, ROWS)]))
        copies = [pltpu.make_async_copy(source, target, sems.at[i]) for i, (source, target) in enumerate(parts)]
        for copy in copies:
            copy.start()
        for copy in copies:
            copy.wait()

    return pl.pallas_call(
        kernel,
        out_shape=jax.ShapeDtypeStruct((16, LONG, PIECE), halo.dtype),
        in_specs=[SMEM] + [ANY] * (1 + len(sources)),
        out_specs=VMEM,
        scratch_shapes=[pltpu.SemaphoreType.DMA((17,))],
        compiler_params=params(),
        cost_estimate=pl.CostEstimate(flops=0, bytes_accessed=4 * LONG * HALF, transcendentals=0),
        name=name,
    )(at[None].astype(jnp.int32), halo, *sources)


def own_tokens(rows, halo):
    def pick(at_ref, refs, i):
        return refs[0].at[:, pl.ds(pl.multiple_of(at_ref[0] * HALF + i * PIECE, PIECE), PIECE)], i

    return in_blocks("own_tokens", pick, halo, lax.axis_index("yh"), rows)


def partner_tokens(nears, fars, halo):
    def pick(at_ref, refs, i):
        place = at_ref[0] * 8 + i if i < 8 else (1 - at_ref[0]) * 8 + i - 8
        begin, piece = i % 8 * PIECE, 0
        if begin >= NEAR[0]:
            begin, piece = begin - NEAR[0], 1
        return refs[i // 8 * 2 + piece].at[:, pl.ds(begin, PIECE)], place

    return in_blocks("partner_tokens", pick, halo, lax.axis_index("core"), *nears, *fars)


def project(own, theirs, places, blocks, first, width, totals=None, final=True, steps=False):
    n_blocks, n_totals = len(blocks), 2 if totals else 0
    origin = blocks[0][3]
    depth = sum(block[2] for block in blocks)

    def kernel(places_ref, *refs):
        token_refs, total_refs, w_refs = refs[:2], refs[2 : 2 + n_totals], refs[2 + n_totals : 2 + n_totals + n_blocks]
        outs, (acc, their_acc, *sides), held, sems = refs[-8:-6], refs[-6:-2], refs[-2], refs[-1]
        accs = (acc, their_acc)
        copies = []
        for i, (_, row, rows, place) in enumerate(blocks):
            begin = place - origin
            parts = [(w_refs[i].at[pl.ds(row, rows), pl.ds(first, width)], held.at[pl.ds(begin, rows)])]
            for side in range(2):
                for k in range(rows // PIECE):
                    parts.append((token_refs[side].at[places_ref[place // PIECE + k]], sides[side].at[begin // PIECE + k]))
            if i == 0 and totals:
                parts += [(total_refs[side], accs[side]) for side in range(2)]
            copies.append([pltpu.make_async_copy(source, target, sems.at[i, n]) for n, (source, target) in enumerate(parts)])
            for copy in copies[i]:
                copy.start()
        for i, (_, row, rows, place) in enumerate(blocks):
            for copy in copies[i]:
                copy.wait()
            begin = place - origin
            w = held[begin : begin + rows]
            for side in range(2):
                lhs = jnp.concatenate([sides[side][begin // PIECE + k] for k in range(rows // PIECE)], axis=1)
                total = jnp.dot(lhs, w, preferred_element_type=F32)
                if i > 0 or totals:
                    total = total + accs[side][...]
                if i < n_blocks - 1:
                    accs[side][...] = total
                elif side == 0 or not final:
                    outs[side][...] = total
                elif steps:
                    outs[1][:, :N] = total[:, :N].astype(BF16)
                    exact = total[:, N:]
                    high = exact.astype(BF16)
                    outs[1][:, N : N + 128] = high
                    outs[1][:, N + 128 :] = (exact - high.astype(F32)).astype(BF16)
                else:
                    outs[1][...] = total.astype(BF16)

    their_width = width + 128 if steps else width
    return pl.pallas_call(
        kernel,
        out_shape=(
            jax.ShapeDtypeStruct((LONG, width), F32),
            jax.ShapeDtypeStruct((LONG, their_width), BF16 if final else F32),
        ),
        in_specs=[SMEM] + [ANY] * (2 + n_totals + n_blocks),
        out_specs=(VMEM, VMEM),
        scratch_shapes=[pltpu.VMEM((LONG, width), F32)] * 2
        + [pltpu.VMEM((depth // PIECE, LONG, PIECE), BF16)] * 2
        + [pltpu.VMEM((depth, width), BF16), pltpu.SemaphoreType.DMA((n_blocks, 11))],
        compiler_params=params(),
        cost_estimate=pl.CostEstimate(flops=4 * LONG * depth * width, bytes_accessed=8_700_000 + 2 * depth * width, transcendentals=0),
        name="project",
    )(places, own, theirs, *(totals or ()), *[block[0] for block in blocks])


def activate(info_ref, projected, taps_ref, bias_ref, first, masked):
    projected = projected.astype(BF16).astype(F32)
    place = info_ref[0] + lax.broadcasted_iota(jnp.int32, projected.shape, 0)
    masked[...] = jnp.where(place >= info_ref[1], projected, 0.0)
    columns = slice(first, first + projected.shape[1])
    total = bias_ref[:, columns]
    for k in range(4):
        total = total + taps_ref[k : k + 1, columns] * masked[pl.ds(HALO - 3 + k, ROWS), :]
    return (total * jax.nn.sigmoid(total)).astype(BF16)


def state_kernel(info_ref, own_ref, other_ref, taps_ref, bias_ref, states_out, steps_out, masked):
    projected = own_ref[:, :N] + other_ref[:, :N].astype(F32)
    states_out[...] = activate(info_ref, projected, taps_ref, bias_ref, HEAD_COLUMNS, masked)
    steps = own_ref[HALO:, N : N + 128] + other_ref[HALO:, N : N + 128].astype(F32) + other_ref[HALO:, N + 128 :].astype(F32)
    steps_out[...] = steps[:, :GROUP_HEADS]


def head_kernel(first_head, info_ref, own_ref, other_ref, taps_ref, bias_ref, weight_ref, states_ref, out_ref, masked):
    projected = own_ref[...] + other_ref[...].astype(F32)
    activated = activate(info_ref, projected, taps_ref, bias_ref, first_head * P_SIZE, masked).astype(F32)
    lane = lax.broadcasted_iota(jnp.int32, (ROWS, 128), 1)
    scaled = []
    for i in range(activated.shape[1] // 128):
        head = first_head + 2 * i
        factor = jnp.where(lane < P_SIZE, weight_ref[:, head : head + 1], weight_ref[:, head + 1 : head + 2])
        scaled.append((activated[:, i * 128 : (i + 1) * 128] * factor).astype(BF16))
    scaled = jnp.concatenate(scaled, axis=1)
    out_ref[...] = lax.dot_general(scaled, states_ref[...], (((0,), (0,)), ((), ())), preferred_element_type=F32)


def call(kernel, out, width, *args):
    return pl.pallas_call(
        kernel,
        out_shape=out,
        in_specs=[SMEM] + [VMEM] * (len(args) - 1),
        out_specs=jax.tree.map(lambda _: VMEM, out),
        scratch_shapes=[pltpu.VMEM((LONG, width), F32)],
        compiler_params=params(),
        cost_estimate=pl.CostEstimate(flops=ROWS * N * width, bytes_accessed=2 * LONG * width, transcendentals=0),
        name="activate",
    )(*args)


def swap(value, axis):
    return lax.ppermute(value, axis, [(0, 1), (1, 0)])


def halos(rows):
    yh = lax.axis_index("yh")
    last = rows[ROWS - HALO :].reshape(HALO, 2, 16, PIECE).transpose(1, 2, 0, 3)
    mine = lax.ppermute(lax.dynamic_index_in_dim(last, yh, 0, False), "z", [(0, 1), (1, 2), (2, 3)])
    pairs = [(y * 4 + z, (1 - y) * 4 + z + 1) for y in range(2) for z in range(3)]
    return mine, lax.ppermute(lax.dynamic_index_in_dim(last, 1 - yh, 0, False), ("yh", "z"), pairs)


def behind(value, by):
    return lax.ppermute(value, "z", [(i, i + by) for i in range(4 - by)])


def saved_rows(near, far, wanted):
    yh, x = lax.axis_index("yh"), lax.axis_index("x")
    found = jnp.zeros((512, N), BF16)
    for i in range(4):
        picked = jnp.zeros((512, N), BF16)
        for side, value in ((yh, near), (1 - yh, far)):
            for b in range(2):
                picked = jnp.where(wanted[i] == 2 * (side * 4 + x) + b, value[b], picked)
        found = found + (shifted(picked, "x", i) if i else picked)
    return found


def all_rows(found):
    z = lax.axis_index("z")
    near = lax.ppermute(found, "z", [(0, 1), (1, 0), (2, 3), (3, 2)])
    two = jnp.where(z % 2 == 0, jnp.concatenate([found, near]), jnp.concatenate([near, found]))
    far = lax.ppermute(two, "z", [(2, 0), (3, 1), (0, 2), (1, 3)])
    return jnp.where(z < 2, jnp.concatenate([two, far]), jnp.concatenate([far, two]))


def per_device(tokens, input_proj, step_proj, conv_weight, conv_bias, step_bias, head_rate, state_pool, resume_slot, offsets):
    yh, x, z, core = (lax.axis_index(a) for a in ("yh", "x", "z", "core"))
    rows = tokens[0]
    info = jnp.stack([z * ROWS - HALO, offsets[0]]).astype(jnp.int32)

    places = jnp.arange(16, dtype=jnp.int32)
    s = jnp.concatenate([input_proj[:, HEAD_COLUMNS:], step_proj, jnp.zeros((PIECE, 96), BF16), input_proj[:, :SPLIT]], axis=1)
    early = lax.all_gather(s, ("x", "z"), axis=0, tiled=True)
    late = lax.all_gather(input_proj[:, SPLIT:HEAD_COLUMNS], ("x", "z"), axis=0, tiled=True)
    half = (1 - yh) * HALF + core * 2048
    projected = {}

    def run(name, array, first):
        steps = name == "states"
        blocks = [(array, j * 1024, 1024, j * 1024) for j in range(4)]
        width = STATE_WIDTH if steps else CHUNKS[name][1]
        own, sent = project(own_side, partner_side, places, blocks, first, width, steps=steps)
        projected[name] = [own, swap(sent, "yh")]
        return own

    def head(name):
        first, width = CHUNKS[name]
        kernel = lambda *refs: head_kernel(first // P_SIZE, *refs)
        out = jax.ShapeDtypeStruct((width, N), F32)
        return call(kernel, out, width, info, *projected[name], conv_weight, conv_bias[None], weight, states)

    first_near = swap(cut(rows, half, NEAR[0]), "yh")
    my_halo, their_halo = halos(rows)
    second_piece, first_near, my_halo, their_halo = together(cut(rows, half + NEAR[0], NEAR[1]), first_near, my_halo, their_halo)
    second_near = swap(second_piece, "yh")
    first_far = swap(first_near, "core")
    own_side = own_tokens(rows, my_halo)
    my_pool = lax.dynamic_slice_in_dim(state_pool, z * 512, 512, 1)
    second_near, first_far, own_side, my_pool = together(second_near, first_far, own_side, my_pool)
    second_far = swap(second_near, "core")
    partner_side = partner_tokens((first_near, second_near), (first_far, second_far), their_halo)
    their_pool = swap(my_pool, "yh")
    partner_side, their_pool, slots = together(partner_side, their_pool, jnp.concatenate([resume_slot, resume_slot]))
    wanted = [resume_slot[0]] + [shifted(slots, "x", -i)[0] for i in (1, 2, 3)]
    early, partner_side, *wanted = together(early, partner_side, *wanted)

    own = run("states", early, 0)
    early, projected["states"][0], my_pool = together(early, own, my_pool)
    found = saved_rows(my_pool, their_pool, wanted)
    own = run("a", early, STATE_WIDTH)
    early, projected["states"][1], projected["a"][0], found = together(early, projected["states"][1], own, found)
    initial = all_rows(found)
    own = run("b", early, STATE_WIDTH + CHUNKS["b"][0])
    projected["b"][0], projected["states"] = together(own, projected["states"])
    out = (jax.ShapeDtypeStruct((ROWS, N), BF16), jax.ShapeDtypeStruct((ROWS, GROUP_HEADS), F32))
    states, step_raw = call(state_kernel, out, N, info, *projected["states"], conv_weight, conv_bias[None])
    valid = (z * ROWS + jnp.arange(ROWS, dtype=jnp.int32) >= offsets[0]).astype(F32)
    step_size = jax.nn.softplus(step_raw + step_bias) * valid[:, None]
    log_decay = -head_rate * step_size
    running = jnp.cumsum(log_decay, axis=0)
    weight = jnp.exp(running[-1:] - running) * step_size
    def columns(array, name):
        return array[CHUNKS[name][0] : sum(CHUNKS[name])]

    def first_steps(own):
        sent = own.astype(BF16)
        return behind(sent, 1), lax.ppermute(sent, "z", [(0, 3)])

    def relayed(one):
        return lax.ppermute(one, "z", [(1, 2), (2, 3)])

    def from_start(name):
        start = jnp.where(z == 0, columns(factor, name) * columns(initial, name).astype(F32), 0.0)
        return head(name) + start

    def all_before(own, name, one, two, three):
        return own + sum(columns(f, name) * came.astype(F32) for f, came in zip(factors, (one, two, three)))

    projected["a"], projected["b"][0] = together(projected["a"], projected["b"][0])
    decay = jnp.exp(running[-1])
    factor = jnp.repeat(decay, P_SIZE)[:, None]
    a = from_start("a")
    a, b_input = together(a, projected["b"])
    projected["b"] = b_input
    one_a, three_a = first_steps(a)
    b = from_start("b")
    late, b, decay = together(late, b, decay)
    own = run("c", late, 0)
    projected["c"][0], one_a, three_a, b, decay = together(own, one_a, three_a, b, decay)
    two_a = relayed(one_a)
    one_b, three_b = first_steps(b)
    decays = lax.all_gather(decay, "z")
    two = decay * lax.dynamic_index_in_dim(decays, (z + 3) % 4, 0, False)
    three = two * lax.dynamic_index_in_dim(decays, (z + 2) % 4, 0, False)
    factors = jnp.repeat(jnp.stack([decay, two, three]), P_SIZE, axis=1)[:, :, None]
    projected["c"][1], two_a, one_b, three_b, factors = together(projected["c"][1], two_a, one_b, three_b, factors)
    two_b = relayed(one_b)
    c = from_start("c")
    one_c, three_c = first_steps(c)
    two_c = relayed(one_c)
    a = all_before(a, "a", one_a, two_a, three_a)
    b = all_before(b, "b", one_b, two_b, three_b)
    c = all_before(c, "c", one_c, two_c, three_c)
    return jnp.concatenate([a, b, c], axis=0)[None, None]


def solution(mesh):
    fine = Mesh(mesh.devices.reshape(2, 4, 4, 2, 2), ("yh", "x", "z", "yl", "core"))
    dp, tensor = ("yh", "x"), ("yl", "core")
    return jax.shard_map(
        per_device,
        mesh=fine,
        in_specs=(
            P(dp, "z", None),
            P(dp + ("z",), tensor),
            P(dp + ("z",), tensor),
            P(None, tensor),
            P(tensor),
            P(tensor),
            P(tensor),
            P(dp, tensor, None),
            P(dp),
            P(dp),
        ),
        out_specs=P(dp, "z", tensor, None),
        check_vma=False,
    )
```

```python
import jax
import jax.numpy as jnp
from jax import lax
from jax.experimental import pallas as pl
from jax.experimental.pallas import tpu as pltpu
from jax.sharding import Mesh
from jax.sharding import PartitionSpec as P

GROUP_HEADS = 32
P_SIZE = 64
N = 256
HALO = 16
ROWS = 512
LONG = ROWS + HALO
PIECE = 256
HALF = 4096
HEAD_COLUMNS = GROUP_HEADS * P_SIZE
F32 = jnp.float32
BF16 = jnp.bfloat16
VMEM_LIMIT = 60 * 1024 * 1024
VMEM = pl.BlockSpec(memory_space=pltpu.VMEM)
SMEM = pl.BlockSpec(memory_space=pltpu.SMEM)
ANY = pl.BlockSpec(memory_space=pltpu.HBM)

CHUNKS = {
    "states": (HEAD_COLUMNS, 256),
    "a": (0, 768),
    "b": (768, 768),
    "c": (1536, 512),
}
SPLIT = 1536
STATE_WIDTH = 384


def together(*values):
    return lax.optimization_barrier(values)


def shifted(part, axis, by):
    return lax.ppermute(part, axis, [(i, (i + by) % 4) for i in range(4)])


def params():
    return pltpu.CompilerParams(vmem_limit_bytes=VMEM_LIMIT)


def pile(parts):
    width = parts[0].shape[1]
    heights = [part.shape[0] for part in parts]

    def kernel(*refs):
        copies = [
            pltpu.make_async_copy(ref, refs[len(parts)].at[pl.ds(sum(heights[:i]), heights[i])], refs[-1].at[i])
            for i, ref in enumerate(refs[: len(parts)])
        ]
        for copy in copies:
            copy.start()
        for copy in copies:
            copy.wait()

    whole = (sum(heights), width)
    return pl.pallas_call(
        kernel,
        out_shape=jax.ShapeDtypeStruct(whole, parts[0].dtype),
        in_specs=[ANY] * len(parts),
        out_specs=VMEM,
        scratch_shapes=[pltpu.SemaphoreType.DMA((len(parts),))],
        compiler_params=params(),
        cost_estimate=pl.CostEstimate(flops=0, bytes_accessed=4 * whole[0] * width, transcendentals=0),
        name="pile",
    )(*parts)


def cut(rows, first, width):
    def kernel(first_ref, rows_ref, out_ref, sem):
        copy = pltpu.make_async_copy(rows_ref.at[:, pl.ds(pl.multiple_of(first_ref[0], PIECE), width)], out_ref, sem)
        copy.start()
        copy.wait()

    return pl.pallas_call(
        kernel,
        out_shape=jax.ShapeDtypeStruct((rows.shape[0], width), rows.dtype),
        in_specs=[SMEM, ANY],
        out_specs=VMEM,
        scratch_shapes=[pltpu.SemaphoreType.DMA],
        compiler_params=params(),
        cost_estimate=pl.CostEstimate(flops=0, bytes_accessed=4 * rows.shape[0] * width, transcendentals=0),
        name="cut",
    )(first[None].astype(jnp.int32), rows)


NEAR = (768, 1280)


def in_blocks(name, pick, halo, at, *sources):
    def kernel(at_ref, halo_ref, *refs):
        out_ref, sems = refs[len(sources) :]
        parts = [(halo_ref, out_ref.at[:, pl.ds(0, HALO)])]
        for i in range(16):
            source, place = pick(at_ref, refs, i)
            parts.append((source, out_ref.at[place, pl.ds(HALO, ROWS)]))
        copies = [pltpu.make_async_copy(source, target, sems.at[i]) for i, (source, target) in enumerate(parts)]
        for copy in copies:
            copy.start()
        for copy in copies:
            copy.wait()

    return pl.pallas_call(
        kernel,
        out_shape=jax.ShapeDtypeStruct((16, LONG, PIECE), halo.dtype),
        in_specs=[SMEM] + [ANY] * (1 + len(sources)),
        out_specs=VMEM,
        scratch_shapes=[pltpu.SemaphoreType.DMA((17,))],
        compiler_params=params(),
        cost_estimate=pl.CostEstimate(flops=0, bytes_accessed=4 * LONG * HALF, transcendentals=0),
        name=name,
    )(at[None].astype(jnp.int32), halo, *sources)


def own_tokens(rows, halo):
    def pick(at_ref, refs, i):
        return refs[0].at[:, pl.ds(pl.multiple_of(at_ref[0] * HALF + i * PIECE, PIECE), PIECE)], i

    return in_blocks("own_tokens", pick, halo, lax.axis_index("yh"), rows)


def partner_tokens(nears, fars, halo):
    def pick(at_ref, refs, i):
        place = at_ref[0] * 8 + i if i < 8 else (1 - at_ref[0]) * 8 + i - 8
        begin, piece = i % 8 * PIECE, 0
        if begin >= NEAR[0]:
            begin, piece = begin - NEAR[0], 1
        return refs[i // 8 * 2 + piece].at[:, pl.ds(begin, PIECE)], place

    return in_blocks("partner_tokens", pick, halo, lax.axis_index("core"), *nears, *fars)


def project(own, theirs, places, blocks, first, width, totals=None, final=True, steps=False):
    n_blocks, n_totals = len(blocks), 2 if totals else 0
    origin = blocks[0][3]
    depth = sum(block[2] for block in blocks)

    def kernel(places_ref, *refs):
        token_refs, total_refs, w_refs = refs[:2], refs[2 : 2 + n_totals], refs[2 + n_totals : 2 + n_totals + n_blocks]
        outs, (acc, their_acc, *sides), held, sems = refs[-8:-6], refs[-6:-2], refs[-2], refs[-1]
        accs = (acc, their_acc)
        copies = []
        for i, (_, row, rows, place) in enumerate(blocks):
            begin = place - origin
            parts = [(w_refs[i].at[pl.ds(row, rows), pl.ds(first, width)], held.at[pl.ds(begin, rows)])]
            for side in range(2):
                for k in range(rows // PIECE):
                    parts.append((token_refs[side].at[places_ref[place // PIECE + k]], sides[side].at[begin // PIECE + k]))
            if i == 0 and totals:
                parts += [(total_refs[side], accs[side]) for side in range(2)]
            copies.append([pltpu.make_async_copy(source, target, sems.at[i, n]) for n, (source, target) in enumerate(parts)])
            for copy in copies[i]:
                copy.start()
        for i, (_, row, rows, place) in enumerate(blocks):
            for copy in copies[i]:
                copy.wait()
            begin = place - origin
            w = held[begin : begin + rows]
            for side in range(2):
                lhs = jnp.concatenate([sides[side][begin // PIECE + k] for k in range(rows // PIECE)], axis=1)
                total = jnp.dot(lhs, w, preferred_element_type=F32)
                if i > 0 or totals:
                    total = total + accs[side][...]
                if i < n_blocks - 1:
                    accs[side][...] = total
                elif side == 0 or not final:
                    outs[side][...] = total
                elif steps:
                    outs[1][:, :N] = total[:, :N].astype(BF16)
                    exact = total[:, N:]
                    high = exact.astype(BF16).astype(F32)
                    outs[1][:, N:] = (high + pltpu.roll(exact - high, GROUP_HEADS, 1)).astype(BF16)
                else:
                    outs[1][...] = total.astype(BF16)

    return pl.pallas_call(
        kernel,
        out_shape=(
            jax.ShapeDtypeStruct((LONG, width), F32),
            jax.ShapeDtypeStruct((LONG, width), BF16 if final else F32),
        ),
        in_specs=[SMEM] + [ANY] * (2 + n_totals + n_blocks),
        out_specs=(VMEM, VMEM),
        scratch_shapes=[pltpu.VMEM((LONG, width), F32)] * 2
        + [pltpu.VMEM((depth // PIECE, LONG, PIECE), BF16)] * 2
        + [pltpu.VMEM((depth, width), BF16), pltpu.SemaphoreType.DMA((n_blocks, 11))],
        compiler_params=params(),
        cost_estimate=pl.CostEstimate(flops=4 * LONG * depth * width, bytes_accessed=8_700_000 + 2 * depth * width, transcendentals=0),
        name="project",
    )(places, own, theirs, *(totals or ()), *[block[0] for block in blocks])


def activate(info_ref, projected, taps_ref, bias_ref, first, masked):
    projected = projected.astype(BF16).astype(F32)
    place = info_ref[0] + lax.broadcasted_iota(jnp.int32, projected.shape, 0)
    masked[...] = jnp.where(place >= info_ref[1], projected, 0.0)
    columns = slice(first, first + projected.shape[1])
    total = bias_ref[:, columns]
    for k in range(4):
        total = total + taps_ref[k : k + 1, columns] * masked[pl.ds(HALO - 3 + k, ROWS), :]
    return (total * jax.nn.sigmoid(total)).astype(BF16)


def state_kernel(info_ref, own_ref, other_ref, taps_ref, bias_ref, states_out, steps_out, masked):
    projected = own_ref[:, :N] + other_ref[:, :N].astype(F32)
    states_out[...] = activate(info_ref, projected, taps_ref, bias_ref, HEAD_COLUMNS, masked)
    sent = other_ref[HALO:, N:].astype(F32)
    steps = own_ref[HALO:, N:] + sent + pltpu.roll(sent, 128 - GROUP_HEADS, 1)
    steps_out[...] = steps[:, :GROUP_HEADS]


def head_kernel(first_head, info_ref, own_ref, other_ref, taps_ref, bias_ref, weight_ref, states_ref, out_ref, masked):
    projected = own_ref[...] + other_ref[...].astype(F32)
    activated = activate(info_ref, projected, taps_ref, bias_ref, first_head * P_SIZE, masked).astype(F32)
    lane = lax.broadcasted_iota(jnp.int32, (ROWS, 128), 1)
    scaled = []
    for i in range(activated.shape[1] // 128):
        head = first_head + 2 * i
        factor = jnp.where(lane < P_SIZE, weight_ref[:, head : head + 1], weight_ref[:, head + 1 : head + 2])
        scaled.append((activated[:, i * 128 : (i + 1) * 128] * factor).astype(BF16))
    scaled = jnp.concatenate(scaled, axis=1)
    out_ref[...] = lax.dot_general(scaled, states_ref[...], (((0,), (0,)), ((), ())), preferred_element_type=F32)


def call(kernel, out, width, *args):
    return pl.pallas_call(
        kernel,
        out_shape=out,
        in_specs=[SMEM] + [VMEM] * (len(args) - 1),
        out_specs=jax.tree.map(lambda _: VMEM, out),
        scratch_shapes=[pltpu.VMEM((LONG, width), F32)],
        compiler_params=params(),
        cost_estimate=pl.CostEstimate(flops=ROWS * N * width, bytes_accessed=2 * LONG * width, transcendentals=0),
        name="activate",
    )(*args)


def swap(value, axis):
    return lax.ppermute(value, axis, [(0, 1), (1, 0)])


def halos(rows):
    yh = lax.axis_index("yh")
    last = rows[ROWS - HALO :].reshape(HALO, 2, 16, PIECE).transpose(1, 2, 0, 3)
    mine = lax.ppermute(lax.dynamic_index_in_dim(last, yh, 0, False), "z", [(0, 1), (1, 2), (2, 3)])
    pairs = [(y * 4 + z, (1 - y) * 4 + z + 1) for y in range(2) for z in range(3)]
    return mine, lax.ppermute(lax.dynamic_index_in_dim(last, 1 - yh, 0, False), ("yh", "z"), pairs)


def behind(value, by):
    return lax.ppermute(value, "z", [(i, i + by) for i in range(4 - by)])


def saved_rows(near, far, wanted):
    yh, x = lax.axis_index("yh"), lax.axis_index("x")
    found = jnp.zeros((512, N), BF16)
    for i in range(4):
        picked = jnp.zeros((512, N), BF16)
        for side, value in ((yh, near), (1 - yh, far)):
            for b in range(2):
                picked = jnp.where(wanted[i] == 2 * (side * 4 + x) + b, value[b], picked)
        found = found + (shifted(picked, "x", i) if i else picked)
    return found


def all_rows(found):
    z = lax.axis_index("z")
    near = lax.ppermute(found, "z", [(0, 1), (1, 0), (2, 3), (3, 2)])
    two = jnp.where(z % 2 == 0, jnp.concatenate([found, near]), jnp.concatenate([near, found]))
    far = lax.ppermute(two, "z", [(2, 0), (3, 1), (0, 2), (1, 3)])
    return jnp.where(z < 2, jnp.concatenate([two, far]), jnp.concatenate([far, two]))


def per_device(tokens, input_proj, step_proj, conv_weight, conv_bias, step_bias, head_rate, state_pool, resume_slot, offsets):
    yh, x, z, core = (lax.axis_index(a) for a in ("yh", "x", "z", "core"))
    rows = tokens[0]
    info = jnp.stack([z * ROWS - HALO, offsets[0]]).astype(jnp.int32)

    places = jnp.arange(16, dtype=jnp.int32)
    s = jnp.concatenate([input_proj[:, HEAD_COLUMNS:], step_proj, jnp.zeros((PIECE, 96), BF16), input_proj[:, :SPLIT]], axis=1)
    early = lax.all_gather(s, ("x", "z"), axis=0, tiled=True)
    late = lax.all_gather(input_proj[:, SPLIT:HEAD_COLUMNS], ("x", "z"), axis=0, tiled=True)
    half = (1 - yh) * HALF + core * 2048
    projected = {}

    def run(name, array, first):
        steps = name == "states"
        blocks = [(array, j * 1024, 1024, j * 1024) for j in range(4)]
        width = STATE_WIDTH if steps else CHUNKS[name][1]
        own, sent = project(own_side, partner_side, places, blocks, first, width, steps=steps)
        projected[name] = [own, swap(sent, "yh")]
        return own

    def head(name):
        first, width = CHUNKS[name]
        kernel = lambda *refs: head_kernel(first // P_SIZE, *refs)
        out = jax.ShapeDtypeStruct((width, N), F32)
        return call(kernel, out, width, info, *projected[name], conv_weight, conv_bias[None], weight, states)

    first_near = swap(cut(rows, half, NEAR[0]), "yh")
    my_halo, their_halo = halos(rows)
    second_piece, first_near, my_halo, their_halo = together(cut(rows, half + NEAR[0], NEAR[1]), first_near, my_halo, their_halo)
    second_near = swap(second_piece, "yh")
    first_far = swap(first_near, "core")
    own_side = own_tokens(rows, my_halo)
    my_pool = lax.dynamic_slice_in_dim(state_pool, z * 512, 512, 1)
    second_near, first_far, own_side, my_pool = together(second_near, first_far, own_side, my_pool)
    second_far = swap(second_near, "core")
    partner_side = partner_tokens((first_near, second_near), (first_far, second_far), their_halo)
    their_pool = swap(my_pool, "yh")
    partner_side, their_pool, slots = together(partner_side, their_pool, jnp.concatenate([resume_slot, resume_slot]))
    wanted = [resume_slot[0]] + [shifted(slots, "x", -i)[0] for i in (1, 2, 3)]
    early, partner_side, *wanted = together(early, partner_side, *wanted)

    own = run("states", early, 0)
    early, projected["states"][0], my_pool = together(early, own, my_pool)
    found = saved_rows(my_pool, their_pool, wanted)
    own = run("a", early, STATE_WIDTH)
    early, projected["states"][1], projected["a"][0], found = together(early, projected["states"][1], own, found)
    initial = all_rows(found)
    out = (jax.ShapeDtypeStruct((ROWS, N), BF16), jax.ShapeDtypeStruct((ROWS, GROUP_HEADS), F32))
    states, step_raw = call(state_kernel, out, N, info, *projected["states"], conv_weight, conv_bias[None])
    valid = (z * ROWS + jnp.arange(ROWS, dtype=jnp.int32) >= offsets[0]).astype(F32)
    step_size = jax.nn.softplus(step_raw + step_bias) * valid[:, None]
    log_decay = -head_rate * step_size
    running = jnp.cumsum(log_decay, axis=0)
    weight = jnp.exp(running[-1:] - running) * step_size
    early, weight, states, running = together(early, weight, states, running)
    own = run("b", early, STATE_WIDTH + CHUNKS["b"][0])
    projected["b"][0] = own
    def columns(array, name):
        return array[CHUNKS[name][0] : sum(CHUNKS[name])]

    def first_step(own, *more):
        return lax.ppermute(jnp.concatenate([own.astype(BF16), *more]), "z", [(0, 1), (1, 0), (2, 3)])

    def second_step(own, came, name):
        mine, its = columns(jnp.where(z == 0, remote, 1.0), name), columns(jnp.where(z == 0, 1.0, factor), name)
        return lax.ppermute((mine * own + its * came.astype(F32)).astype(BF16), "z", [(1, 2), (0, 3)])

    def from_start(name):
        start = jnp.where(z == 0, columns(factor, name) * columns(initial, name).astype(F32), 0.0)
        return head(name) + start

    def all_before(own, name, one, two):
        for_one, for_two = jnp.where(z == 0, 0.0, factor), jnp.where(z == 3, factor * remote, factor)
        return own + columns(for_one, name) * one.astype(F32) + columns(for_two, name) * two.astype(F32)

    projected["a"], projected["b"][0] = together(projected["a"], projected["b"][0])
    decay = jnp.exp(running[-1])
    factor = jnp.repeat(decay, P_SIZE)[:, None]
    a = from_start("a")
    high = decay.astype(BF16)
    terms = jnp.concatenate([high, (decay - high.astype(F32)).astype(BF16), jnp.zeros(N - 2 * GROUP_HEADS, BF16)])
    one_a = first_step(a, jnp.broadcast_to(terms, (16, N)))
    late, one_a, decay = together(late, one_a, decay)
    own = run("c", late, 0)
    projected["c"][0], projected["b"], one_a = together(own, projected["b"], one_a)
    width = CHUNKS["a"][1]
    remote = one_a[width, :GROUP_HEADS].astype(F32) + one_a[width, GROUP_HEADS : 2 * GROUP_HEADS].astype(F32)
    remote = jnp.repeat(remote, P_SIZE)[:, None]
    one_a = one_a[:width]
    two_a = second_step(a, one_a, "a")
    b = from_start("b")
    one_b = first_step(b)
    projected["c"][1], two_a, one_b = together(projected["c"][1], two_a, one_b)
    two_b = second_step(b, one_b, "b")
    c = from_start("c")
    one_c = first_step(c)
    two_c = second_step(c, one_c, "c")
    a = all_before(a, "a", one_a, two_a)
    b = all_before(b, "b", one_b, two_b)
    c = all_before(c, "c", one_c, two_c)
    return jnp.concatenate([a, b, c], axis=0)[None, None]


def solution(mesh):
    fine = Mesh(mesh.devices.reshape(2, 4, 4, 2, 2), ("yh", "x", "z", "yl", "core"))
    dp, tensor = ("yh", "x"), ("yl", "core")
    return jax.shard_map(
        per_device,
        mesh=fine,
        in_specs=(
            P(dp, "z", None),
            P(dp + ("z",), tensor),
            P(dp + ("z",), tensor),
            P(None, tensor),
            P(tensor),
            P(tensor),
            P(tensor),
            P(dp, tensor, None),
            P(dp),
            P(dp),
        ),
        out_specs=P(dp, "z", tensor, None),
        check_vma=False,
    )
```

```python
import jax
import jax.numpy as jnp
from jax import lax
from jax.experimental import pallas as pl
from jax.experimental.pallas import tpu as pltpu
from jax.sharding import Mesh
from jax.sharding import PartitionSpec as P

GROUP_HEADS = 32
P_SIZE = 64
N = 256
HALO = 16
ROWS = 512
LONG = ROWS + HALO
PIECE = 256
HALF = 4096
HEAD_COLUMNS = GROUP_HEADS * P_SIZE
F32 = jnp.float32
BF16 = jnp.bfloat16
VMEM_LIMIT = 60 * 1024 * 1024
VMEM = pl.BlockSpec(memory_space=pltpu.VMEM)
SMEM = pl.BlockSpec(memory_space=pltpu.SMEM)
ANY = pl.BlockSpec(memory_space=pltpu.HBM)

CHUNKS = {
    "states": (HEAD_COLUMNS, 256),
    "a": (0, 896),
    "b": (896, 768),
    "c": (1664, 384),
}
SPLIT = 1664
STATE_WIDTH = 384


def together(*values):
    return lax.optimization_barrier(values)


def shifted(part, axis, by):
    return lax.ppermute(part, axis, [(i, (i + by) % 4) for i in range(4)])


def params():
    return pltpu.CompilerParams(vmem_limit_bytes=VMEM_LIMIT)


def pile(parts):
    width = parts[0].shape[1]
    heights = [part.shape[0] for part in parts]

    def kernel(*refs):
        copies = [
            pltpu.make_async_copy(ref, refs[len(parts)].at[pl.ds(sum(heights[:i]), heights[i])], refs[-1].at[i])
            for i, ref in enumerate(refs[: len(parts)])
        ]
        for copy in copies:
            copy.start()
        for copy in copies:
            copy.wait()

    whole = (sum(heights), width)
    return pl.pallas_call(
        kernel,
        out_shape=jax.ShapeDtypeStruct(whole, parts[0].dtype),
        in_specs=[ANY] * len(parts),
        out_specs=VMEM,
        scratch_shapes=[pltpu.SemaphoreType.DMA((len(parts),))],
        compiler_params=params(),
        cost_estimate=pl.CostEstimate(flops=0, bytes_accessed=4 * whole[0] * width, transcendentals=0),
        name="pile",
    )(*parts)


def cut(rows, first, width):
    def kernel(first_ref, rows_ref, out_ref, sem):
        copy = pltpu.make_async_copy(rows_ref.at[:, pl.ds(pl.multiple_of(first_ref[0], PIECE), width)], out_ref, sem)
        copy.start()
        copy.wait()

    return pl.pallas_call(
        kernel,
        out_shape=jax.ShapeDtypeStruct((rows.shape[0], width), rows.dtype),
        in_specs=[SMEM, ANY],
        out_specs=VMEM,
        scratch_shapes=[pltpu.SemaphoreType.DMA],
        compiler_params=params(),
        cost_estimate=pl.CostEstimate(flops=0, bytes_accessed=4 * rows.shape[0] * width, transcendentals=0),
        name="cut",
    )(first[None].astype(jnp.int32), rows)


NEAR = (768, 1280)


def in_blocks(name, pick, halo, at, *sources):
    def kernel(at_ref, halo_ref, *refs):
        out_ref, sems = refs[len(sources) :]
        parts = [(halo_ref, out_ref.at[:, pl.ds(0, HALO)])]
        for i in range(16):
            source, place = pick(at_ref, refs, i)
            parts.append((source, out_ref.at[place, pl.ds(HALO, ROWS)]))
        copies = [pltpu.make_async_copy(source, target, sems.at[i]) for i, (source, target) in enumerate(parts)]
        for copy in copies:
            copy.start()
        for copy in copies:
            copy.wait()

    return pl.pallas_call(
        kernel,
        out_shape=jax.ShapeDtypeStruct((16, LONG, PIECE), halo.dtype),
        in_specs=[SMEM] + [ANY] * (1 + len(sources)),
        out_specs=VMEM,
        scratch_shapes=[pltpu.SemaphoreType.DMA((17,))],
        compiler_params=params(),
        cost_estimate=pl.CostEstimate(flops=0, bytes_accessed=4 * LONG * HALF, transcendentals=0),
        name=name,
    )(at[None].astype(jnp.int32), halo, *sources)


def own_tokens(rows, halo):
    def pick(at_ref, refs, i):
        return refs[0].at[:, pl.ds(pl.multiple_of(at_ref[0] * HALF + i * PIECE, PIECE), PIECE)], i

    return in_blocks("own_tokens", pick, halo, lax.axis_index("yh"), rows)


def partner_tokens(nears, fars, halo):
    def pick(at_ref, refs, i):
        place = at_ref[0] * 8 + i if i < 8 else (1 - at_ref[0]) * 8 + i - 8
        begin, piece = i % 8 * PIECE, 0
        if begin >= NEAR[0]:
            begin, piece = begin - NEAR[0], 1
        return refs[i // 8 * 2 + piece].at[:, pl.ds(begin, PIECE)], place

    return in_blocks("partner_tokens", pick, halo, lax.axis_index("core"), *nears, *fars)


def project(own, theirs, places, blocks, first, width, totals=None, final=True, steps=False):
    n_blocks, n_totals = len(blocks), 2 if totals else 0
    origin = blocks[0][3]
    depth = sum(block[2] for block in blocks)

    def kernel(places_ref, *refs):
        token_refs, total_refs, w_refs = refs[:2], refs[2 : 2 + n_totals], refs[2 + n_totals : 2 + n_totals + n_blocks]
        outs, (acc, their_acc, *sides), held, sems = refs[-8:-6], refs[-6:-2], refs[-2], refs[-1]
        accs = (acc, their_acc)
        copies = []
        for i, (_, row, rows, place) in enumerate(blocks):
            begin = place - origin
            parts = [(w_refs[i].at[pl.ds(row, rows), pl.ds(first, width)], held.at[pl.ds(begin, rows)])]
            for side in range(2):
                for k in range(rows // PIECE):
                    parts.append((token_refs[side].at[places_ref[place // PIECE + k]], sides[side].at[begin // PIECE + k]))
            if i == 0 and totals:
                parts += [(total_refs[side], accs[side]) for side in range(2)]
            copies.append([pltpu.make_async_copy(source, target, sems.at[i, n]) for n, (source, target) in enumerate(parts)])
            for copy in copies[i]:
                copy.start()
        for i, (_, row, rows, place) in enumerate(blocks):
            for copy in copies[i]:
                copy.wait()
            begin = place - origin
            w = held[begin : begin + rows]
            for side in range(2):
                lhs = jnp.concatenate([sides[side][begin // PIECE + k] for k in range(rows // PIECE)], axis=1)
                total = jnp.dot(lhs, w, preferred_element_type=F32)
                if i > 0 or totals:
                    total = total + accs[side][...]
                if i < n_blocks - 1:
                    accs[side][...] = total
                elif side == 0 or not final:
                    outs[side][...] = total
                elif steps:
                    outs[1][:, :N] = total[:, :N].astype(BF16)
                    exact = total[:, N:]
                    high = exact.astype(BF16).astype(F32)
                    outs[1][:, N:] = (high + pltpu.roll(exact - high, GROUP_HEADS, 1)).astype(BF16)
                else:
                    outs[1][...] = total.astype(BF16)

    return pl.pallas_call(
        kernel,
        out_shape=(
            jax.ShapeDtypeStruct((LONG, width), F32),
            jax.ShapeDtypeStruct((LONG, width), BF16 if final else F32),
        ),
        in_specs=[SMEM] + [ANY] * (2 + n_totals + n_blocks),
        out_specs=(VMEM, VMEM),
        scratch_shapes=[pltpu.VMEM((LONG, width), F32)] * 2
        + [pltpu.VMEM((depth // PIECE, LONG, PIECE), BF16)] * 2
        + [pltpu.VMEM((depth, width), BF16), pltpu.SemaphoreType.DMA((n_blocks, 11))],
        compiler_params=params(),
        cost_estimate=pl.CostEstimate(flops=4 * LONG * depth * width, bytes_accessed=8_700_000 + 2 * depth * width, transcendentals=0),
        name="project",
    )(places, own, theirs, *(totals or ()), *[block[0] for block in blocks])


def activate(info_ref, projected, taps_ref, bias_ref, first, masked):
    projected = projected.astype(BF16).astype(F32)
    place = info_ref[0] + lax.broadcasted_iota(jnp.int32, projected.shape, 0)
    masked[...] = jnp.where(place >= info_ref[1], projected, 0.0)
    columns = slice(first, first + projected.shape[1])
    total = bias_ref[:, columns]
    for k in range(4):
        total = total + taps_ref[k : k + 1, columns] * masked[pl.ds(HALO - 3 + k, ROWS), :]
    return (total * jax.nn.sigmoid(total)).astype(BF16)


def state_kernel(info_ref, own_ref, other_ref, taps_ref, bias_ref, states_out, steps_out, masked):
    projected = own_ref[:, :N] + other_ref[:, :N].astype(F32)
    states_out[...] = activate(info_ref, projected, taps_ref, bias_ref, HEAD_COLUMNS, masked)
    sent = other_ref[HALO:, N:].astype(F32)
    steps = own_ref[HALO:, N:] + sent + pltpu.roll(sent, 128 - GROUP_HEADS, 1)
    steps_out[...] = steps[:, :GROUP_HEADS]


def head_kernel(first_head, info_ref, own_ref, other_ref, taps_ref, bias_ref, weight_ref, states_ref, out_ref, masked):
    projected = own_ref[...] + other_ref[...].astype(F32)
    activated = activate(info_ref, projected, taps_ref, bias_ref, first_head * P_SIZE, masked).astype(F32)
    lane = lax.broadcasted_iota(jnp.int32, (ROWS, 128), 1)
    scaled = []
    for i in range(activated.shape[1] // 128):
        head = first_head + 2 * i
        factor = jnp.where(lane < P_SIZE, weight_ref[:, head : head + 1], weight_ref[:, head + 1 : head + 2])
        scaled.append((activated[:, i * 128 : (i + 1) * 128] * factor).astype(BF16))
    scaled = jnp.concatenate(scaled, axis=1)
    out_ref[...] = lax.dot_general(scaled, states_ref[...], (((0,), (0,)), ((), ())), preferred_element_type=F32)


def call(kernel, out, width, *args):
    return pl.pallas_call(
        kernel,
        out_shape=out,
        in_specs=[SMEM] + [VMEM] * (len(args) - 1),
        out_specs=jax.tree.map(lambda _: VMEM, out),
        scratch_shapes=[pltpu.VMEM((LONG, width), F32)],
        compiler_params=params(),
        cost_estimate=pl.CostEstimate(flops=ROWS * N * width, bytes_accessed=2 * LONG * width, transcendentals=0),
        name="activate",
    )(*args)


def swap(value, axis):
    return lax.ppermute(value, axis, [(0, 1), (1, 0)])


def halos(rows):
    yh = lax.axis_index("yh")
    last = rows[ROWS - HALO :].reshape(HALO, 2, 16, PIECE).transpose(1, 2, 0, 3)
    mine = lax.ppermute(lax.dynamic_index_in_dim(last, yh, 0, False), "z", [(0, 1), (1, 2), (2, 3)])
    pairs = [(y * 4 + z, (1 - y) * 4 + z + 1) for y in range(2) for z in range(3)]
    return mine, lax.ppermute(lax.dynamic_index_in_dim(last, 1 - yh, 0, False), ("yh", "z"), pairs)


def behind(value, by):
    return lax.ppermute(value, "z", [(i, i + by) for i in range(4 - by)])


def saved_rows(near, far, wanted):
    yh, x = lax.axis_index("yh"), lax.axis_index("x")
    found = jnp.zeros((512, N), BF16)
    for i in range(4):
        picked = jnp.zeros((512, N), BF16)
        for side, value in ((yh, near), (1 - yh, far)):
            for b in range(2):
                picked = jnp.where(wanted[i] == 2 * (side * 4 + x) + b, value[b], picked)
        found = found + (shifted(picked, "x", i) if i else picked)
    return found


def all_rows(found):
    z = lax.axis_index("z")
    near = lax.ppermute(found, "z", [(0, 1), (1, 0), (2, 3), (3, 2)])
    two = jnp.where(z % 2 == 0, jnp.concatenate([found, near]), jnp.concatenate([near, found]))
    far = lax.ppermute(two, "z", [(2, 0), (3, 1), (0, 2), (1, 3)])
    return jnp.where(z < 2, jnp.concatenate([two, far]), jnp.concatenate([far, two]))


def per_device(tokens, input_proj, step_proj, conv_weight, conv_bias, step_bias, head_rate, state_pool, resume_slot, offsets):
    yh, x, z, core = (lax.axis_index(a) for a in ("yh", "x", "z", "core"))
    rows = tokens[0]
    info = jnp.stack([z * ROWS - HALO, offsets[0]]).astype(jnp.int32)

    places = jnp.arange(16, dtype=jnp.int32)
    s = jnp.concatenate([input_proj[:, HEAD_COLUMNS:], step_proj, jnp.zeros((PIECE, 96), BF16), input_proj[:, :SPLIT]], axis=1)
    early = lax.all_gather(s, ("x", "z"), axis=0, tiled=True)
    late = lax.all_gather(input_proj[:, SPLIT:HEAD_COLUMNS], ("x", "z"), axis=0, tiled=True)
    half = (1 - yh) * HALF + core * 2048
    projected = {}

    def run(name, array, first):
        steps = name == "states"
        blocks = [(array, j * 1024, 1024, j * 1024) for j in range(4)]
        width = STATE_WIDTH if steps else CHUNKS[name][1]
        own, sent = project(own_side, partner_side, places, blocks, first, width, steps=steps)
        projected[name] = [own, swap(sent, "yh")]
        return own

    def head(name):
        first, width = CHUNKS[name]
        kernel = lambda *refs: head_kernel(first // P_SIZE, *refs)
        out = jax.ShapeDtypeStruct((width, N), F32)
        return call(kernel, out, width, info, *projected[name], conv_weight, conv_bias[None], weight, states)

    first_near = swap(cut(rows, half, NEAR[0]), "yh")
    my_halo, their_halo = halos(rows)
    second_piece, first_near, my_halo, their_halo = together(cut(rows, half + NEAR[0], NEAR[1]), first_near, my_halo, their_halo)
    second_near = swap(second_piece, "yh")
    first_far = swap(first_near, "core")
    own_side = own_tokens(rows, my_halo)
    my_pool = lax.dynamic_slice_in_dim(state_pool, z * 512, 512, 1)
    second_near, first_far, own_side, my_pool = together(second_near, first_far, own_side, my_pool)
    second_far = swap(second_near, "core")
    partner_side = partner_tokens((first_near, second_near), (first_far, second_far), their_halo)
    their_pool = swap(my_pool, "yh")
    partner_side, their_pool, slots = together(partner_side, their_pool, jnp.concatenate([resume_slot, resume_slot]))
    wanted = [resume_slot[0]] + [shifted(slots, "x", -i)[0] for i in (1, 2, 3)]
    early, partner_side, *wanted = together(early, partner_side, *wanted)

    own = run("states", early, 0)
    early, projected["states"][0], my_pool = together(early, own, my_pool)
    found = saved_rows(my_pool, their_pool, wanted)
    own = run("a", early, STATE_WIDTH)
    early, projected["states"][1], projected["a"][0], found = together(early, projected["states"][1], own, found)
    initial = all_rows(found)
    out = (jax.ShapeDtypeStruct((ROWS, N), BF16), jax.ShapeDtypeStruct((ROWS, GROUP_HEADS), F32))
    states, step_raw = call(state_kernel, out, N, info, *projected["states"], conv_weight, conv_bias[None])
    valid = (z * ROWS + jnp.arange(ROWS, dtype=jnp.int32) >= offsets[0]).astype(F32)
    step_size = jax.nn.softplus(step_raw + step_bias) * valid[:, None]
    log_decay = -head_rate * step_size
    running = jnp.cumsum(log_decay, axis=0)
    weight = jnp.exp(running[-1:] - running) * step_size
    early, weight, states, running = together(early, weight, states, running)
    own = run("b", early, STATE_WIDTH + CHUNKS["b"][0])
    projected["b"][0] = own
    def columns(array, name):
        return array[CHUNKS[name][0] : sum(CHUNKS[name])]

    def first_step(own, *more):
        return lax.ppermute(jnp.concatenate([own.astype(BF16), *more]), "z", [(0, 1), (1, 0), (2, 3)])

    def second_step(own, came, name):
        mine, its = columns(jnp.where(z == 0, remote, 1.0), name), columns(jnp.where(z == 0, 1.0, factor), name)
        return lax.ppermute((mine * own + its * came.astype(F32)).astype(BF16), "z", [(1, 2), (0, 3)])

    def from_start(name):
        start = jnp.where(z == 0, columns(factor, name) * columns(initial, name).astype(F32), 0.0)
        return head(name) + start

    def all_before(own, name, one, two):
        for_one, for_two = jnp.where(z == 0, 0.0, factor), jnp.where(z == 3, factor * remote, factor)
        return own + columns(for_one, name) * one.astype(F32) + columns(for_two, name) * two.astype(F32)

    projected["a"], projected["b"][0] = together(projected["a"], projected["b"][0])
    decay = jnp.exp(running[-1])
    factor = jnp.repeat(decay, P_SIZE)[:, None]
    a = from_start("a")
    high = decay.astype(BF16)
    terms = jnp.concatenate([high, (decay - high.astype(F32)).astype(BF16), jnp.zeros(N - 2 * GROUP_HEADS, BF16)])
    one_a = first_step(a, jnp.broadcast_to(terms, (16, N)))
    late, one_a, decay = together(late, one_a, decay)
    own = run("c", late, 0)
    projected["c"][0], projected["b"], one_a = together(own, projected["b"], one_a)
    width = CHUNKS["a"][1]
    remote = one_a[width, :GROUP_HEADS].astype(F32) + one_a[width, GROUP_HEADS : 2 * GROUP_HEADS].astype(F32)
    remote = jnp.repeat(remote, P_SIZE)[:, None]
    one_a = one_a[:width]
    two_a = second_step(a, one_a, "a")
    b = from_start("b")
    one_b = first_step(b)
    projected["c"][1], two_a, one_b = together(projected["c"][1], two_a, one_b)
    two_b = second_step(b, one_b, "b")
    c = from_start("c")
    one_c = first_step(c)
    two_c = second_step(c, one_c, "c")
    a = all_before(a, "a", one_a, two_a)
    b = all_before(b, "b", one_b, two_b)
    c = all_before(c, "c", one_c, two_c)
    return jnp.concatenate([a, b, c], axis=0)[None, None]


def solution(mesh):
    fine = Mesh(mesh.devices.reshape(2, 4, 4, 2, 2), ("yh", "x", "z", "yl", "core"))
    dp, tensor = ("yh", "x"), ("yl", "core")
    return jax.shard_map(
        per_device,
        mesh=fine,
        in_specs=(
            P(dp, "z", None),
            P(dp + ("z",), tensor),
            P(dp + ("z",), tensor),
            P(None, tensor),
            P(tensor),
            P(tensor),
            P(tensor),
            P(dp, tensor, None),
            P(dp),
            P(dp),
        ),
        out_specs=P(dp, "z", tensor, None),
        check_vma=False,
    )
```
